128 devices in a mesh: wide: 64 (over z, y, x), narrow: 2 (over core).
Axes of the slice: x: 4, y: 4, z: 4, core: 2. Of those that a mesh axis runs over, the one named last changes fastest.
Arguments:
- cache: bfloat16 [512, 1024, 576], P('wide'), may hold values from -4 to 4
- lengths: int32 [512], P('wide'), may hold values from 0 to 1020, as said below
- mig_send: int32 [64, 2, 8], P('wide'), may hold values from 0 to 255, as said below
- mig_recv: int32 [64, 2, 8], P('wide'), may hold values from 0 to 255, as said below
- mig_count: int32 [64, 2], P('wide'), may hold values from 2 to 8, as said below
- queries: bfloat16 [4, 512, 128, 576], P(None, 'wide', 'narrow'), may hold values from -25 to 25
- new_latent: bfloat16 [4, 512, 576], P(None, 'wide'), may hold values from -4 to 4
- tokens: bfloat16 [4, 512, 7168], P(None, 'wide', 'narrow'), may hold values from -6 to 6
- expert_ids: int32 [4, 512, 8], P(None, 'wide'), may hold values from 0 to 31, all different within a row; in each aligned block of 8 rows (0 to 7, 8 to 15, ..., all dimensions but the last counted through in order) at most 4 rows name the same one
- affinity: float32 [4, 512, 8], P(None, 'wide'), may hold values from 0.05 to 1
- gate_weight: bfloat16 [7168, 32768], P('narrow', 'wide'), may hold values from -0.0625 to 0.0625
- up_weight: bfloat16 [7168, 32768], P('narrow', 'wide'), may hold values from -0.0625 to 0.0625
- down_weight: bfloat16 [32768, 7168], P('wide', 'narrow'), may hold values from -0.1875 to 0.1875
Outputs:
- context: bfloat16 [4, 512, 128, 512], P(None, 'wide', 'narrow')
- moe_out: bfloat16 [4, 512, 7168], P(None, 'wide', 'narrow')
The draws below stay inside these ranges and needn't reach their ends.
Inputs may be any that keep to these rules, and one draw needn't show every extreme that they name: `lengths`: each rank sends one request to each of the two ranks after it; the slots that it sends from hold 0, the two slots that receive hold the arriving request's length, between 64 and 256, and every rank has a slot of length 1020. `mig_count`: entry [d, j] is the arriving request's length over 32 rounded up; one entry is 8 in every draw. `mig_send`: entry [s, j, k] is block k of the slot that rank s sends to rank s + j + 1; the two slots of a rank differ. `mig_recv`: entry [d, j, k] is block k of the slot of rank d that receives from rank d - j - 1; the two receiving slots of a rank differ from each other and from its sending slots. `expert_ids`: the 8 rows of one wide rank at one step name one expert at most 4 times.
All inputs are finite; a program needn't handle non-finite values.
Results may differ from the reference program's by a relative error of at most 0.0057.
Values may be sent and summed in bfloat16 or wider, within the bound.
No kernel may reach another device: no remote copies, remote signals or barrier semaphores. Data moves between devices by JAX's collectives and lax.ppermute only.
A program may use at most 128 MiB of HBM per device.

```python
import math
import jax
import jax.numpy as jnp
import numpy as np
from jax import lax

D = 7168
HEADS = 128
LAT = 512
ROPE = 64
FF = 1024
TOPK = 8
STEPS = 4
BLK = 32
PB = 8
REQ = 8
CAP = 1024
SLOTS = 512
EXPERTS = 32
MOST = 4
N_WIDE = 64


def migration_plan(key):
    per_slot = CAP // BLK
    slot_keys = jax.random.split(jax.random.fold_in(key, 201), N_WIDE)
    orders = jax.vmap(lambda one_key: jax.random.permutation(one_key, REQ))(slot_keys).astype(jnp.int32)
    out_slots = orders[:, 0:2]
    in_slots = orders[:, 2:4]
    full_slot = orders[:, 4]
    low_len = max(1, PB * BLK // 4)
    moved_len = jax.random.randint(jax.random.fold_in(key, 203), (N_WIDE, 2), low_len, PB * BLK + 1, dtype=jnp.int32)
    moved_len = moved_len.at[0, 0].set(PB * BLK)
    heavy = jax.random.randint(jax.random.fold_in(key, 208), (N_WIDE, 1), 0, 2, dtype=jnp.int32)
    long_len = jax.random.randint(jax.random.fold_in(key, 204), (N_WIDE, REQ), CAP // 2, CAP - STEPS + 1, dtype=jnp.int32)
    short_len = jax.random.randint(jax.random.fold_in(key, 205), (N_WIDE, REQ), 1, CAP // 4 + 1, dtype=jnp.int32)
    other_len = jnp.where(heavy == 1, long_len, short_len)
    ranks = jnp.arange(N_WIDE, dtype=jnp.int32)
    len_first = moved_len[(ranks - 1) % N_WIDE, 0]
    len_second = moved_len[(ranks - 2) % N_WIDE, 1]
    slot_ids = jnp.arange(REQ, dtype=jnp.int32)[None, :]
    lengths = jnp.where(slot_ids == full_slot[:, None], CAP - STEPS, other_len)
    lengths = jnp.where(slot_ids == in_slots[:, 0:1], len_first[:, None], lengths)
    lengths = jnp.where(slot_ids == in_slots[:, 1:2], len_second[:, None], lengths)
    lengths = jnp.where(slot_ids == out_slots[:, 0:1], 0, lengths)
    lengths = jnp.where(slot_ids == out_slots[:, 1:2], 0, lengths)
    block_steps = jnp.arange(PB, dtype=jnp.int32)[None, None, :]
    send_table = out_slots[:, :, None] * per_slot + block_steps
    recv_table = in_slots[:, :, None] * per_slot + block_steps
    arriving = jnp.stack([len_first, len_second], axis=1)
    counts = (arriving + BLK - 1) // BLK
    return (lengths.reshape(-1).astype(jnp.int32), send_table.astype(jnp.int32), recv_table.astype(jnp.int32), counts.astype(jnp.int32))


def draw_lengths(key, part):
    tables = migration_plan(key)
    return tables[0]


def draw_mig_send(key, part):
    tables = migration_plan(key)
    return tables[1]


def draw_mig_recv(key, part):
    tables = migration_plan(key)
    return tables[2]


def draw_mig_count(key, part):
    tables = migration_plan(key)
    return tables[3]


def latent_pieces(key):
    noise = jnp.clip(jax.random.normal(jax.random.fold_in(key, 101), (STEPS, SLOTS, LAT + ROPE), jnp.float32), -4.0, 4.0)
    return noise


def mixed_latent(noise):
    return noise


def draw_new_latent(key, part):
    noise = latent_pieces(key)
    latent = mixed_latent(noise)
    return latent.astype(jnp.bfloat16)


def draw_queries(key, part):
    noise = latent_pieces(key)
    key = jax.random.fold_in(key, 6)
    shape = (STEPS, SLOTS, HEADS, LAT + ROPE)
    latent = mixed_latent(noise)
    own = jnp.clip(jax.random.normal(jax.random.fold_in(key, 1), shape, jnp.float32), -4.0, 4.0)
    values = own + 0.15 * latent[:, :, None, :]
    return values.astype(jnp.bfloat16)


def levels(own_key, shape, shards, smallest, largest):
    def one(axis_at, parts):
        heights = jax.random.uniform(jax.random.fold_in(jax.random.fold_in(own_key, 6), axis_at), (parts,), jnp.float32, smallest / len(shards), largest / len(shards))
        return jnp.repeat(jnp.exp(heights), shape[axis_at] // parts).reshape((-1,) + (1,) * (len(shape) - axis_at - 1))

    factor_of = one(*shards[0])
    for cut in shards[1:]:
        factor_of = factor_of * one(*cut)
    return factor_of


def deal_out(rng, own, number, rows, count, top, reach, slope):
    ranking = jax.random.permutation(rng, count)
    packed, common = shares(count, rows * top, reach, slope, True), shares(count, rows * top, reach, slope, False)
    places = jnp.arange(count)

    def named(sizes, turn):
        used = int((sizes > 0).sum())
        fixed = max(1, used // 4)
        moved = fixed + (places - fixed + turn * (used - fixed)) % max(1, count - fixed)
        return jnp.zeros((count,), jnp.int32).at[ranking[jnp.where(places < fixed, places, moved)]].set(jnp.asarray(sizes, jnp.int32))

    sizes = jnp.where(number % 4 == 0, named(packed, number // 4), named(common, number - number // 4 - 1))
    mixed = jax.random.permutation(jax.random.fold_in(own, 3), count)
    donor, sink = mixed[0:count // 2 * 2:2], mixed[1:count // 2 * 2:2]
    margin = jnp.minimum(sizes[donor] - 1, reach - sizes[sink]) // 2
    margin = jnp.where((donor == ranking[0]) | (sink == ranking[0]) | (sizes[sink] == 0), 0, jnp.maximum(margin, 0))
    moved = jax.random.randint(jax.random.fold_in(own, 4), (count // 2,), 0, 1 << 20) % (margin + 1)
    sizes = sizes.at[donor].add(-moved).at[sink].add(moved)
    labels = jnp.searchsorted(jnp.cumsum(sizes), jnp.arange(rows * top), side="right").astype(jnp.int32)
    grid = labels.reshape(top, rows).T
    grid = grid[jax.random.permutation(jax.random.fold_in(own, 1), rows)]
    turn = jax.random.randint(jax.random.fold_in(own, 2), (rows, 1), 0, top)
    return jnp.take_along_axis(grid, (jnp.arange(top)[None, :] + turn) % top, axis=1)


def shares(count, total, most, skew, full):
    loads = [(1 << 20) // math.isqrt(standing ** skew) + 1 for standing in range(1, count + 1)]
    largest = most if full else min(most, max(-(-total // count), total * loads[0] // sum(loads)))
    least = 1 if total - largest >= count - 1 else 0
    holding, rest = [largest] + [least] * (count - 1), total - largest - least * (count - 1)
    while rest > 0:
        free = [i for i in range(1, count) if holding[i] < largest] or [i for i in range(1, count) if holding[i] < most]
        whole, remaining = sum([loads[i] for i in free]), rest
        for i in free:
            addition = min(most - holding[i], max(1, remaining * loads[i] // whole), rest)
            holding[i] = holding[i] + addition
            rest = rest - addition
    return np.array(holding)


def normal_values(key, extent, scale, bound, cuts=(), kind=jnp.bfloat16):
    result = jax.random.normal(key, extent, jnp.float32) * scale
    if len(cuts) > 0:
        result = levels(key, extent, cuts, -0.22, 0.18) * result
    return jnp.clip(result, min=-bound, max=bound).astype(kind)


def setup_inputs(seed: int = 0) -> dict:
    seeds = jax.random.split(jax.random.key(seed), 14)
    cache = normal_values(seeds[0], (SLOTS, CAP, LAT + ROPE), 1.0, 4.0, ((0, 64),))
    lengths = draw_lengths(jax.random.fold_in(seeds[13], 71), 0)
    mig_send = draw_mig_send(jax.random.fold_in(seeds[13], 71), 0)
    mig_recv = draw_mig_recv(jax.random.fold_in(seeds[13], 71), 0)
    mig_count = draw_mig_count(jax.random.fold_in(seeds[13], 71), 0)
    queries = draw_queries(jax.random.fold_in(seeds[13], 71), 0)
    new_latent = draw_new_latent(jax.random.fold_in(seeds[13], 71), 0)
    tokens = normal_values(seeds[7], (STEPS, SLOTS, D), 1.0, 6.0, ((1, 64), (2, 2)))
    expert_ids_keys = jax.random.split(jax.random.fold_in(seeds[8], 1), STEPS * SLOTS // REQ)
    expert_ids_turns = jax.random.permutation(jax.random.fold_in(seeds[8], 3), STEPS * SLOTS // REQ)
    expert_ids = jax.vmap(lambda own, number: deal_out(jax.random.fold_in(seeds[8], 2), own, number, REQ, EXPERTS, TOPK, MOST, 2))(expert_ids_keys, expert_ids_turns).reshape((STEPS, SLOTS, TOPK))
    affinity = jnp.clip(jnp.exp(math.log(1.0) - 2.9957323 * jax.random.uniform(seeds[9], (STEPS, SLOTS, TOPK), jnp.float32) ** levels(seeds[9], (STEPS, SLOTS, TOPK), ((1, 64),), -0.2, 0.2)), 0.05, 1.0)
    gate_weight = normal_values(seeds[10], (D, EXPERTS * FF), D ** -0.5, 0.0625, ((0, 2), (1, 64)))
    up_weight = normal_values(seeds[11], (D, EXPERTS * FF), D ** -0.5, 0.0625, ((0, 2), (1, 64)))
    down_weight = normal_values(seeds[12], (EXPERTS * FF, D), FF ** -0.5, 0.1875, ((0, 64), (1, 2)))
    return dict(cache=cache, lengths=lengths, mig_send=mig_send, mig_recv=mig_recv, mig_count=mig_count, queries=queries, new_latent=new_latent, tokens=tokens, expert_ids=expert_ids, affinity=affinity, gate_weight=gate_weight, up_weight=up_weight, down_weight=down_weight)


score_scale = 192.0 ** -0.5
route_scale = 2.5


def migrate(cache, mig_send, mig_recv, mig_count):
    width = LAT + ROPE
    per_rank = REQ * (CAP // BLK)
    blocks = cache.reshape(N_WIDE * per_rank, BLK, width)
    ranks = jnp.arange(N_WIDE, dtype=jnp.int32)[:, None]
    hop_index = jnp.arange(2, dtype=jnp.int32)[None, :]
    dest = ((ranks + hop_index + 1) % N_WIDE).astype(jnp.int32)
    source = (mig_send + (ranks * per_rank)[:, :, None]).astype(jnp.int32)
    recv_at = mig_recv[dest, hop_index]
    count_at = mig_count[dest, hop_index]
    target = (recv_at + (dest * per_rank)[:, :, None]).astype(jnp.int32)
    is_live = jnp.arange(PB, dtype=jnp.int32)[None, None, :] < count_at[:, :, None]
    target = jnp.where(is_live, target, N_WIDE * per_rank).astype(jnp.int32)
    picked = blocks[source.reshape(-1)]
    moved = blocks.at[target.reshape(-1)].set(picked, mode="drop")
    return moved.reshape(cache.shape)


def attend(queries, cache, lengths, fresh_keys):
    query_wide = queries.astype(jnp.float32)
    cache_wide = cache.astype(jnp.float32)
    fresh_wide = fresh_keys.astype(jnp.float32)
    past_scores = jnp.einsum("rhc,rkc->rhk", query_wide, cache_wide, precision=lax.Precision.HIGHEST) * score_scale
    positions = lax.broadcasted_iota(jnp.int32, past_scores.shape, 2)
    past_scores = jnp.where(positions < lengths[:, None, None], past_scores, -jnp.inf)
    fresh_scores = jnp.einsum("rhc,rkc->rhk", query_wide, fresh_wide, precision=lax.Precision.HIGHEST) * score_scale
    peak_score = jnp.maximum(jnp.max(past_scores, axis=2), jnp.max(fresh_scores, axis=2))[..., None]
    past_exp = jnp.exp(past_scores - peak_score)
    fresh_exp = jnp.exp(fresh_scores - peak_score)
    denominator = jnp.sum(past_exp, axis=2, keepdims=True) + jnp.sum(fresh_exp, axis=2, keepdims=True)
    past_weights = (past_exp / denominator).astype(jnp.bfloat16).astype(jnp.float32)
    fresh_weights = (fresh_exp / denominator).astype(jnp.bfloat16).astype(jnp.float32)
    context = jnp.einsum("rhk,rkc->rhc", past_weights, cache_wide[:, :, :LAT], precision=lax.Precision.HIGHEST)
    context = context + jnp.einsum("rhk,rkc->rhc", fresh_weights, fresh_wide[:, :, :LAT], precision=lax.Precision.HIGHEST)
    return context.astype(jnp.bfloat16)


def rank_attend(pieces):
    return attend(pieces[0], pieces[1], pieces[2], pieces[3])


def expert_step(step_tokens, step_ids, step_affinity, gate_weight, up_weight, down_weight):
    route_share = route_scale * step_affinity / jnp.sum(step_affinity, axis=2, keepdims=True)
    onehot = (step_ids[..., None] == jnp.arange(EXPERTS, dtype=jnp.int32)).astype(jnp.int32)
    flat_hot = onehot.reshape(N_WIDE, REQ * TOPK, EXPERTS)
    earlier = jnp.cumsum(flat_hot, axis=1) - flat_hot
    position = jnp.sum(earlier * flat_hot, axis=2).reshape(N_WIDE, REQ, TOPK)
    cell = (step_ids * MOST + position).astype(jnp.int32)
    matches = cell[..., None] == jnp.arange(EXPERTS * MOST, dtype=jnp.int32)
    row_index = jnp.arange(REQ, dtype=jnp.int32)[None, :, None, None]
    row_of = jnp.sum(jnp.where(matches, row_index, 0), axis=(1, 2)).astype(jnp.int32)
    is_used = jnp.any(matches, axis=(1, 2))
    mixing = jnp.sum(jnp.where(matches, route_share[..., None], jnp.float32(0.0)), axis=2)
    padded = jnp.concatenate([step_tokens, jnp.zeros((N_WIDE, 1, D), step_tokens.dtype)], axis=1)
    index = jnp.where(is_used, row_of, REQ).astype(jnp.int32)
    gathered = padded[jnp.arange(N_WIDE, dtype=jnp.int32)[:, None], index]
    buckets = jnp.swapaxes(gathered.reshape(N_WIDE, EXPERTS, MOST, D), 0, 1).reshape(EXPERTS, N_WIDE * MOST, D)
    half_units = FF // 2

    def one_expert(running, inputs):
        rows, expert = inputs
        start = (expert * FF).astype(jnp.int32)
        gate = jnp.dot(rows, lax.dynamic_slice_in_dim(gate_weight, start, FF, 1), preferred_element_type=jnp.float32)
        up_act = jnp.dot(rows, lax.dynamic_slice_in_dim(up_weight, start, FF, 1), preferred_element_type=jnp.float32)
        hidden = (jax.nn.silu(gate) * up_act).astype(jnp.bfloat16)
        lower = jnp.dot(hidden[:, :half_units], lax.dynamic_slice_in_dim(down_weight, start, half_units, 0), preferred_element_type=jnp.float32).astype(jnp.bfloat16)
        upper = jnp.dot(hidden[:, half_units:], lax.dynamic_slice_in_dim(down_weight, (start + half_units).astype(jnp.int32), half_units, 0), preferred_element_type=jnp.float32).astype(jnp.bfloat16)
        both = (lower.astype(jnp.float32) + upper.astype(jnp.float32)).reshape(N_WIDE, MOST, D)
        part_weight = lax.dynamic_slice_in_dim(mixing, (expert * MOST).astype(jnp.int32), MOST, 2)
        running = running + jnp.einsum("wrm,wmd->wrd", part_weight, both, precision=lax.Precision.HIGHEST)
        return running, None

    initial = jnp.zeros((N_WIDE, REQ, D), jnp.float32)
    summed, unused = lax.scan(one_expert, initial, (buckets, jnp.arange(EXPERTS, dtype=jnp.int32)))
    return summed.astype(jnp.bfloat16).reshape(SLOTS, D)


def reference(cache, lengths, mig_send, mig_recv, mig_count, queries, new_latent, tokens, expert_ids, affinity, gate_weight, up_weight, down_weight):
    width = LAT + ROPE
    moved = migrate(cache, mig_send, mig_recv, mig_count)
    ranked_cache = moved.reshape(N_WIDE, REQ, CAP, width)
    ranked_lengths = lengths.reshape(N_WIDE, REQ)
    contexts = []
    outputs = []
    for step_index in range(STEPS):
        fresh_keys = jnp.swapaxes(new_latent[: step_index + 1], 0, 1).reshape(N_WIDE, REQ, step_index + 1, width)
        ranked_queries = queries[step_index].reshape(N_WIDE, REQ, HEADS, width)
        step_context = lax.map(rank_attend, (ranked_queries, ranked_cache, ranked_lengths, fresh_keys))
        contexts.append(step_context.reshape(SLOTS, HEADS, LAT))
        outputs.append(expert_step(tokens[step_index].reshape(N_WIDE, REQ, D), expert_ids[step_index].reshape(N_WIDE, REQ, TOPK), affinity[step_index].reshape(N_WIDE, REQ, TOPK), gate_weight, up_weight, down_weight))
    return jnp.stack(contexts), jnp.stack(outputs)
```

```python
import functools

import jax
import jax.numpy as jnp
from jax import lax
from jax.experimental import pallas as pl
from jax.experimental.pallas import tpu as pltpu
from jax.sharding import PartitionSpec as P

LAT = 512
STEPS = 4
MOST = 4
SIDE = 4
RANKS = SIDE * SIDE
MOVED = 256
TILE = 512
BATCHES = ((0, 1), (2, 3))
ORDERS = ((("x", "y", "z"), ("x", "z", "y")), (("y", "x", "z"), ("z", "x", "y")))
BACKS = ORDERS[::-1]
STRIDE = {"z": 16, "y": 4, "x": 1}
BOTH = ("wide", "narrow")
VMEM = 28 * 1024 * 1024

score_scale = 192.0 ** (-0.5)
route_scale = 2.5


def params(**more):
    return pltpu.CompilerParams(vmem_limit_bytes=VMEM, **more)


def moved_along(rank, axis, steps):
    place = rank // STRIDE[axis] % SIDE
    return rank + ((place + steps) % SIDE - place) * STRIDE[axis]


def hop(value, axes, steps):
    if steps == 0:
        return value
    pairs = [
        (rank * 2 + core, moved_along(rank, axes[core], steps) * 2 + core)
        for rank in range(64)
        for core in range(2)
    ]
    return lax.ppermute(value, BOTH, pairs)


def axes_at(orders, stage):
    return tuple(order[stage] for order in orders)


def attend_kernel(lengths, receivers, query_ref, cache_ref, moved_ref, fresh_ref, out_ref):
    slot = pl.program_id(0)
    length = lengths[slot]
    blocks = (length + 255) // 256
    steps, _, heads, width = query_ref.shape
    rows = steps * heads
    contract_last = (((1,), (1,)), ((), ()))

    def run(count):
        query = query_ref[...].reshape(rows, width)
        fresh = fresh_ref[0]
        fresh_scores = (
            lax.dot_general(query, fresh, contract_last, preferred_element_type=jnp.float32)
            * score_scale
        )
        row_step = lax.broadcasted_iota(jnp.int32, fresh_scores.shape, 0) // heads
        column = lax.broadcasted_iota(jnp.int32, fresh_scores.shape, 1)
        fresh_scores = jnp.where(column <= row_step, fresh_scores, -jnp.inf)
        peak = jnp.max(fresh_scores, axis=1, keepdims=True)
        keys = []
        scores = []
        for index in range(count):
            key = cache_ref[0, :, index * 256 : (index + 1) * 256]
            if count == 1:
                key = jnp.where(slot == receivers[0], moved_ref[0], key)
                key = jnp.where(slot == receivers[1], moved_ref[1], key)
            score = jnp.dot(query, key, preferred_element_type=jnp.float32) * score_scale
            if index == count - 1:
                position = lax.broadcasted_iota(jnp.int32, score.shape, 1) + index * 256
                score = jnp.where(position < length, score, -jnp.inf)
            peak = jnp.maximum(peak, jnp.max(score, axis=1, keepdims=True))
            keys.append(key)
            scores.append(score)
        fresh_exp = jnp.exp(fresh_scores - peak)
        total = jnp.sum(fresh_exp, axis=1, keepdims=True)
        exps = []
        for score in scores:
            weight = jnp.exp(score - peak)
            total = total + jnp.sum(weight, axis=1, keepdims=True)
            exps.append(weight)
        inverse = 1.0 / total
        context = jnp.dot(
            (fresh_exp * inverse).astype(jnp.bfloat16),
            fresh[:, :LAT],
            preferred_element_type=jnp.float32,
        )
        for weight, key in zip(exps, keys):
            context = context + lax.dot_general(
                (weight * inverse).astype(jnp.bfloat16),
                key[:LAT],
                contract_last,
                preferred_element_type=jnp.float32,
            )
        out_ref[...] = context.astype(jnp.bfloat16).reshape(out_ref.shape)

    for count in range(5):
        pl.when(blocks == count)(functools.partial(run, count))


def attend(queries, cache, lengths, receivers, moved, new_latent):
    steps, slots, heads, width = queries.shape
    fresh = jnp.pad(jnp.swapaxes(new_latent, 0, 1), ((0, 0), (0, 16 - steps), (0, 0)))
    return pl.pallas_call(
        attend_kernel,
        grid_spec=pltpu.PrefetchScalarGridSpec(
            num_scalar_prefetch=2,
            grid=(slots,),
            in_specs=[
                pl.BlockSpec((steps, 1, heads, width), lambda i, *_: (0, i, 0, 0)),
                pl.BlockSpec((1, width, cache.shape[2]), lambda i, *_: (i, 0, 0)),
                pl.BlockSpec(moved.shape, lambda i, *_: (0, 0, 0)),
                pl.BlockSpec((1, 16, width), lambda i, *_: (i, 0, 0)),
            ],
            out_specs=pl.BlockSpec((steps, 1, heads, LAT), lambda i, *_: (0, i, 0, 0)),
        ),
        out_shape=jax.ShapeDtypeStruct((steps, slots, heads, LAT), jnp.bfloat16),
        compiler_params=params(),
        cost_estimate=pl.CostEstimate(
            flops=2 * 18 * 256 * 256 * 1280, bytes_accessed=14_000_000, transcendentals=18 * 256 * 256
        ),
        name="attend",
    )(lengths, receivers, queries, cache, moved, fresh)


def pack_kernel(token_ref, id_ref, affinity_ref, *out_refs):
    steps, requests, half_width = token_ref.shape
    topk = id_ref.shape[2]
    rows = steps * requests
    ids = id_ref[...].reshape(rows, topk)
    affinity = affinity_ref[...].reshape(rows, topk)
    share = route_scale * affinity / jnp.sum(affinity, axis=1, keepdims=True)
    high = share.astype(jnp.bfloat16).astype(jnp.float32)
    low = share - high
    lane = lax.broadcasted_iota(jnp.int32, (rows, 128), 1)
    hot = jnp.zeros((rows, 128), jnp.float32)
    shares = jnp.zeros((rows, 128), jnp.float32)
    for k in range(topk):
        named = ids[:, k : k + 1]
        hot = jnp.where(lane == named, 1.0, hot)
        shares = jnp.where(lane == named + 32, high[:, k : k + 1], shares)
        shares = jnp.where(lane == named + 64, low[:, k : k + 1], shares)
    row = lax.broadcasted_iota(jnp.int32, (rows, rows), 0)
    other = lax.broadcasted_iota(jnp.int32, (rows, rows), 1)
    earlier = ((other < row) & (row // requests == other // requests)).astype(jnp.bfloat16)
    before = jnp.dot(earlier, hot.astype(jnp.bfloat16), preferred_element_type=jnp.float32)
    routing = jnp.where(lane < 32, jnp.where(hot > 0.5, before, -1.0), shares).astype(jnp.bfloat16)
    features = token_ref[...].reshape(rows, half_width)
    start = 0
    for out_ref in out_refs:
        count = out_ref.shape[0]
        out_ref[:, :half_width] = features[start : start + count]
        out_ref[:, half_width:] = routing[start : start + count]
        start += count


def pack(tokens, expert_ids, affinity):
    steps, requests, half_width = tokens.shape
    return pl.pallas_call(
        pack_kernel,
        out_shape=[
            jax.ShapeDtypeStruct((len(batch) * requests, half_width + 128), jnp.bfloat16) for batch in BATCHES
        ],
        name="pack",
    )(tokens, expert_ids, affinity)


def along_lanes(aux, wanted, shape, transposed):
    if transposed:
        lane = lax.broadcasted_iota(jnp.int32, (shape[0], 128), 1)
        chosen = (lane == wanted).astype(jnp.bfloat16)
        return lax.dot_general(
            chosen, aux, (((1,), (1,)), ((), ())), preferred_element_type=jnp.float32
        )
    lane = lax.broadcasted_iota(jnp.int32, (128, shape[1]), 0)
    chosen = (lane == wanted).astype(jnp.bfloat16)
    return jnp.dot(aux, chosen, preferred_element_type=jnp.float32)


def placed(aux, expert, shape, transposed):
    place = along_lanes(aux, expert, shape, transposed).astype(jnp.int32)
    row = lax.broadcasted_iota(jnp.int32, shape, 1 if transposed else 0)
    cell = lax.broadcasted_iota(jnp.int32, shape, 0 if transposed else 1)
    return (place >= 0) & (row // 8 * MOST + place == cell)


def pick_kernel(experts, *refs):
    piece_refs, out_refs = refs[:4], refs[4:8]
    cells, half_width = out_refs[0].shape
    aux = jnp.concatenate([ref[:, half_width:] for ref in piece_refs], axis=0)
    pickers = [
        placed(aux, experts[index], (cells, aux.shape[0]), True).astype(jnp.bfloat16)
        for index in range(SIDE)
    ]
    for start in range(0, half_width, TILE):
        rows = jnp.concatenate([ref[:, start : start + TILE] for ref in piece_refs], axis=0)
        for index in range(SIDE):
            out_refs[index][:, start : start + TILE] = jnp.dot(
                pickers[index], rows, preferred_element_type=jnp.float32
            ).astype(jnp.bfloat16)


IN_SMEM = pl.BlockSpec(memory_space=pltpu.SMEM)
IN_VMEM = pl.BlockSpec(memory_space=pltpu.VMEM)


def pick(experts, pieces, half_width):
    rows = pieces[0].shape[0] * SIDE
    cells = rows // 2
    return pl.pallas_call(
        pick_kernel,
        in_specs=[IN_SMEM] + [IN_VMEM] * SIDE,
        out_specs=[IN_VMEM] * SIDE,
        out_shape=[jax.ShapeDtypeStruct((cells, half_width), jnp.bfloat16)] * SIDE,
        compiler_params=params(),
        cost_estimate=pl.CostEstimate(
            flops=2 * SIDE * cells * rows * half_width,
            bytes_accessed=2 * (SIDE * cells + rows) * half_width,
            transcendentals=0,
        ),
        name="pick",
    )(experts, *pieces)


def mix_kernel(by_inner, experts, *refs):
    piece_refs, cell_refs, out_refs = refs[:4], refs[4:8], refs[8:12]
    cells, half_width = cell_refs[0].shape
    rows_each = out_refs[0].shape[0]
    rows = rows_each * SIDE
    each = rows_each // SIDE
    aux = jnp.concatenate([ref[:, half_width:] for ref in piece_refs], axis=0)
    mixers = []
    for index in range(SIDE):
        chosen = placed(aux, experts[index], (rows, cells), False)
        for part in range(2):
            share = along_lanes(aux, experts[index] + 32 * (part + 1), (rows, cells), False)
            mixers.append(jnp.where(chosen, share, 0.0).astype(jnp.bfloat16))
    high = jnp.concatenate(mixers[0::2], axis=1)
    low = jnp.concatenate(mixers[1::2], axis=1)
    for start in range(0, half_width, TILE):
        answers = jnp.concatenate([ref[:, start : start + TILE] for ref in cell_refs], axis=0)
        mixed = jnp.dot(high, answers, preferred_element_type=jnp.float32)
        mixed = mixed + jnp.dot(low, answers, preferred_element_type=jnp.float32)
        mixed = mixed.astype(jnp.bfloat16)
        for outer in range(SIDE):
            for inner in range(SIDE):
                block = mixed[(outer * SIDE + inner) * each : (outer * SIDE + inner + 1) * each]
                piece, place = (inner, outer) if by_inner else (outer, inner)
                out_refs[piece][place * each : (place + 1) * each, start : start + TILE] = block


def mix(experts, pieces, answers, by_inner):
    rows_each = pieces[0].shape[0]
    rows = rows_each * SIDE
    cells, half_width = answers[0].shape
    return pl.pallas_call(
        functools.partial(mix_kernel, by_inner),
        in_specs=[IN_SMEM] + [IN_VMEM] * 2 * SIDE,
        out_specs=[IN_VMEM] * SIDE,
        out_shape=[jax.ShapeDtypeStruct((rows_each, half_width), jnp.bfloat16)] * SIDE,
        compiler_params=params(),
        cost_estimate=pl.CostEstimate(
            flops=2 * 2 * SIDE * cells * rows * half_width,
            bytes_accessed=2 * (SIDE * cells + rows) * half_width,
            transcendentals=0,
        ),
        name="mix",
    )(experts, *pieces, *answers)


def widen_kernel(strides, *refs):
    row_refs, gate_ref, up_ref, out_gate, out_up = refs[:4], *refs[4:]
    cells = row_refs[0].shape[0]
    each = cells // RANKS
    units = gate_ref.shape[1]
    rows = jnp.concatenate([ref[...] for ref in row_refs], axis=0)
    for weight_ref, out_ref in ((gate_ref, out_gate), (up_ref, out_up)):
        for start in range(0, units, 256):
            part = jnp.dot(
                rows, weight_ref[:, start : start + 256], preferred_element_type=jnp.float32
            )
            for outer in range(SIDE):
                for middle in range(SIDE):
                    for inner in range(SIDE):
                        block = (outer * SIDE + middle) * SIDE + inner
                        place = outer * strides[0] + middle * strides[1] + inner * strides[2]
                        place = pl.multiple_of(place * each, each)
                        out_ref[pl.ds(place, each), start : start + 256] = part[
                            block * each : (block + 1) * each
                        ]


def widen(strides, rows, gate_weight, up_weight):
    cells, half_width = rows[0].shape
    units = gate_weight.shape[1]
    total = SIDE * cells
    return pl.pallas_call(
        widen_kernel,
        in_specs=[IN_SMEM] + [IN_VMEM] * (SIDE + 2),
        out_specs=[IN_VMEM] * 2,
        out_shape=[jax.ShapeDtypeStruct((total, units), jnp.float32)] * 2,
        compiler_params=params(),
        cost_estimate=pl.CostEstimate(
            flops=4 * total * half_width * units,
            bytes_accessed=2 * (total + 2 * units) * half_width + 8 * total * units,
            transcendentals=0,
        ),
        name="widen",
    )(strides, *rows, gate_weight, up_weight)


def narrow_kernel(strides, *refs):
    gate_own, gate_other, up_own, up_other, weight_ref = refs[:5]
    out_refs, hidden = refs[5:9], refs[9]
    cells, half_width = out_refs[0].shape
    each = cells // RANKS
    for outer in range(SIDE):
        for middle in range(SIDE):
            parts = []
            for inner in range(SIDE):
                place = outer * strides[0] + middle * strides[1] + inner * strides[2]
                place = pl.ds(pl.multiple_of(place * each, each), each)
                gate = gate_own[place, :] + gate_other[place, :]
                up = up_own[place, :] + up_other[place, :]
                parts.append(gate / (1.0 + jnp.exp(-gate)) * up)
            block = (outer * SIDE + middle) * SIDE
            hidden[block * each : (block + SIDE) * each, :] = jnp.concatenate(
                parts, axis=0
            ).astype(jnp.bfloat16)
    for start in range(0, half_width, TILE):
        result = jnp.dot(
            hidden[...], weight_ref[:, start : start + TILE], preferred_element_type=jnp.float32
        )
        for index in range(SIDE):
            out_refs[index][:, start : start + TILE] = result[
                index * cells : (index + 1) * cells
            ].astype(jnp.bfloat16)


def narrow(strides, gate_own, gate_other, up_own, up_other, down_weight):
    total, units = gate_own.shape
    cells = total // SIDE
    half_width = down_weight.shape[1]
    return pl.pallas_call(
        narrow_kernel,
        in_specs=[IN_SMEM] + [IN_VMEM] * 5,
        out_specs=[IN_VMEM] * SIDE,
        out_shape=[jax.ShapeDtypeStruct((cells, half_width), jnp.bfloat16)] * SIDE,
        scratch_shapes=[pltpu.VMEM((total, units), jnp.bfloat16)],
        compiler_params=params(),
        cost_estimate=pl.CostEstimate(
            flops=2 * total * half_width * units,
            bytes_accessed=2 * (total + units) * half_width + 16 * total * units,
            transcendentals=total * units,
        ),
        name="narrow",
    )(strides, gate_own, gate_other, up_own, up_other, down_weight)


def swap_cores(value):
    return lax.ppermute(value, "narrow", [(0, 1), (1, 0)])


def add_up(values):
    total = values[0].astype(jnp.float32)
    for value in values[1:]:
        total = total + value.astype(jnp.float32)
    return total.astype(jnp.bfloat16)


def body(
    cache,
    lengths,
    mig_send,
    mig_recv,
    mig_count,
    queries,
    new_latent,
    tokens,
    expert_ids,
    affinity,
    gate_weight,
    up_weight,
    down_weight,
):
    core = lax.axis_index("narrow")
    rank = lax.axis_index("wide")
    slot_count, capacity, width = cache.shape
    per_slot = capacity // 32
    requests, half_width = tokens.shape[1:]

    keys_last = jnp.swapaxes(cache, 1, 2)
    sending = mig_send[0, core, 0] // per_slot
    outgoing = lax.dynamic_slice(keys_last, (sending, 0, 0), (1, width, MOVED))[0]
    pairs = [(r * 2 + j, (r + j + 1) % 64 * 2 + j) for r in range(64) for j in range(2)]
    arrived = lax.ppermute(outgoing, BOTH, pairs)
    arrived_other = swap_cores(arrived)
    receivers = jnp.stack([mig_recv[0, core, 0], mig_recv[0, 1 - core, 0]]) // per_slot
    moved = jnp.stack([arrived, arrived_other])

    reach = []
    for steps in range(SIDE):
        by_core = [moved_along(rank, ORDERS[0][c][2], steps) // 2 for c in range(2)]
        reach.append(jnp.where(core == 0, by_core[0], by_core[1]))
    experts = jnp.stack(reach).astype(jnp.int32)
    scale = {"z": 16, "y": 4, "x": 1}

    own_rows = pack(tokens, expert_ids, affinity)
    gathered = []
    for index in range(len(BATCHES)):
        orders = ORDERS[index]
        first = [hop(own_rows[index], axes_at(orders, 0), steps) for steps in range(SIDE)]
        plane_row = jnp.concatenate(first, axis=0)
        gathered.append([hop(plane_row, axes_at(orders, 1), steps) for steps in range(SIDE)])
    picked = []
    for index in range(len(BATCHES)):
        if index == 1:
            context = attend(queries, keys_last, lengths, receivers, moved, new_latent)
            gathered[1], context = lax.optimization_barrier((gathered[1], context))
        rows = pick(experts, gathered[index], half_width)
        picked.append([hop(rows[steps], axes_at(ORDERS[index], 2), steps) for steps in range(SIDE)])

    outputs = []
    for index, (pieces, rows) in enumerate(zip(gathered, picked)):
        orders, backs = ORDERS[index], BACKS[index]
        by_core = [[scale[axis] for axis in order[::-1]] for order in orders]
        strides = jnp.where(
            core == 0, jnp.array(by_core[0], jnp.int32), jnp.array(by_core[1], jnp.int32)
        )
        gate, up = widen(strides, rows, gate_weight, up_weight)
        answers = narrow(strides, gate, swap_cores(gate), up, swap_cores(up), down_weight)
        answers = [hop(answers[steps], axes_at(orders, 2), -steps) for steps in range(SIDE)]
        mixed = mix(experts, pieces, answers, backs[0][1] == orders[0][0])
        mixed = add_up([hop(mixed[steps], axes_at(backs, 1), -steps) for steps in range(SIDE)])
        mixed = mixed.reshape(SIDE, -1, half_width)
        outputs.append(
            add_up([hop(mixed[steps], axes_at(backs, 0), -steps) for steps in range(SIDE)])
        )
    moe_out = jnp.concatenate(outputs, axis=0).reshape(STEPS, requests, half_width)
    return (context, moe_out)


def solution(mesh):
    specs = (
        P("wide", None, None),
        P("wide"),
        P("wide", None, None),
        P("wide", None, None),
        P("wide", None),
        P(None, "wide", "narrow", None),
        P(None, "wide", None),
        P(None, "wide", "narrow"),
        P(None, "wide", None),
        P(None, "wide", None),
        P("narrow", "wide"),
        P("narrow", "wide"),
        P("wide", "narrow"),
    )
    return jax.shard_map(
        body,
        mesh=mesh,
        in_specs=specs,
        out_specs=(P(None, "wide", "narrow", None), P(None, "wide", "narrow")),
        check_vma=False,
    )
```

```python
import functools

import jax
import jax.numpy as jnp
from jax import lax
from jax.experimental import pallas as pl
from jax.experimental.pallas import tpu as pltpu
from jax.sharding import PartitionSpec as P

LAT = 512
STEPS = 4
MOST = 4
SIDE = 4
RANKS = SIDE * SIDE
MOVED = 256
TILE = 512
BATCHES = ((0, 1), (2, 3))
ORDERS = (("x", "y", "z"), ("x", "z", "y"))
STRIDE = {"z": 16, "y": 4, "x": 1}
BOTH = ("wide", "narrow")
MIB = 1024 * 1024
SHARE = 0.1


def cost(micros):
    return pl.CostEstimate(flops=int(micros * SHARE * 1.1e9), bytes_accessed=1, transcendentals=0)


IN_VMEM = pl.BlockSpec(memory_space=pltpu.VMEM)

score_scale = 192.0 ** (-0.5)
route_scale = 2.5


def params(mib):
    return pltpu.CompilerParams(vmem_limit_bytes=mib * MIB)


def moved_along(rank, axis, steps):
    place = rank // STRIDE[axis] % SIDE
    return rank + ((place + steps) % SIDE - place) * STRIDE[axis]


def hop(value, axes, steps):
    if steps == 0:
        return value
    pairs = [
        (rank * 2 + core, moved_along(rank, axes[core], steps) * 2 + core)
        for rank in range(64)
        for core in range(2)
    ]
    return lax.ppermute(value, BOTH, pairs)


def axes_at(stage):
    return tuple(order[stage] for order in ORDERS)


def by_core(core, first, second):
    return jnp.where(core == 0, first, second)


def reached_experts():
    rank, core = lax.axis_index("wide"), lax.axis_index("narrow")
    first, second = axes_at(2)
    return [
        by_core(core, moved_along(rank, first, steps) // 2, moved_along(rank, second, steps) // 2)
        for steps in range(SIDE)
    ]


def block_strides():
    core = lax.axis_index("narrow")
    return [by_core(core, *(STRIDE[axis] for axis in axes_at(level))) for level in (2, 1, 0)]


def attend_kernel(
    lengths, receivers, query_hbm, cache_hbm, moved_ref, other_ref, fresh_ref, out_ref, query_held, cache_held, sems
):
    slot = pl.program_id(0)
    count = pl.num_programs(0)

    def copies(index):
        held = lax.rem(index, 2)
        return (
            pltpu.make_async_copy(query_hbm.at[:, index], query_held.at[held], sems.at[held, 0]),
            pltpu.make_async_copy(cache_hbm.at[index], cache_held.at[held], sems.at[held, 1]),
        )

    @pl.when(slot == 0)
    def _():
        for copy in copies(slot):
            copy.start()

    @pl.when(slot + 1 < count)
    def _():
        for copy in copies(slot + 1):
            copy.start()

    for copy in copies(slot):
        copy.wait()
    now = lax.rem(slot, 2)
    query_ref, cache_ref = query_held.at[now], cache_held.at[now]
    length = lengths[slot]
    blocks = (length + 255) // 256
    steps, heads, width = query_ref.shape
    rows = steps * heads
    slots = fresh_ref.shape[1]
    core = lax.axis_index("narrow")
    per_slot = cache_ref.shape[1] // 32
    contract_last = (((1,), (1,)), ((), ()))

    def run(count):
        query = query_ref[...].reshape(rows, width)
        fresh = fresh_ref[...].reshape(-1, width)
        fresh_scores = (
            lax.dot_general(query, fresh, contract_last, preferred_element_type=jnp.float32)
            * score_scale
        )
        row_step = lax.broadcasted_iota(jnp.int32, fresh_scores.shape, 0) // heads
        column = lax.broadcasted_iota(jnp.int32, fresh_scores.shape, 1)
        allowed = (column // slots <= row_step) & (column % slots == slot)
        fresh_scores = jnp.where(allowed, fresh_scores, -jnp.inf)
        peak = jnp.max(fresh_scores, axis=1, keepdims=True)
        keys = []
        scores = []
        for index in range(count):
            key = cache_ref[:, index * 256 : (index + 1) * 256]
            if count == 1:
                key = jnp.where(slot == receivers[core, 0] // per_slot, moved_ref[...], key)
                key = jnp.where(slot == receivers[1 - core, 0] // per_slot, other_ref[...], key)
            score = jnp.dot(query, key, preferred_element_type=jnp.float32) * score_scale
            if index == count - 1:
                position = lax.broadcasted_iota(jnp.int32, score.shape, 1) + index * 256
                score = jnp.where(position < length, score, -jnp.inf)
            peak = jnp.maximum(peak, jnp.max(score, axis=1, keepdims=True))
            keys.append(key)
            scores.append(score)
        fresh_exp = jnp.exp(fresh_scores - peak)
        total = jnp.sum(fresh_exp, axis=1, keepdims=True)
        exps = []
        for score in scores:
            weight = jnp.exp(score - peak)
            total = total + jnp.sum(weight, axis=1, keepdims=True)
            exps.append(weight)
        inverse = 1.0 / total
        context = jnp.dot(
            (fresh_exp * inverse).astype(jnp.bfloat16),
            fresh[:, :LAT],
            preferred_element_type=jnp.float32,
        )
        for weight, key in zip(exps, keys):
            context = context + lax.dot_general(
                (weight * inverse).astype(jnp.bfloat16),
                key[:LAT],
                contract_last,
                preferred_element_type=jnp.float32,
            )
        out_ref[...] = context.astype(jnp.bfloat16).reshape(out_ref.shape)

    for count in range(5):
        pl.when(blocks == count)(functools.partial(run, count))


def attend(queries, cache, lengths, receivers, moved, other, new_latent):
    steps, slots, heads, width = queries.shape
    in_place = pl.BlockSpec(memory_space=pltpu.HBM)
    return pl.pallas_call(
        attend_kernel,
        grid_spec=pltpu.PrefetchScalarGridSpec(
            num_scalar_prefetch=2,
            grid=(slots,),
            in_specs=[in_place, in_place, IN_VMEM, IN_VMEM, IN_VMEM],
            out_specs=pl.BlockSpec((steps, 1, heads, LAT), lambda i, *_: (0, i, 0, 0)),
            scratch_shapes=[
                pltpu.VMEM((2, steps, heads, width), jnp.bfloat16),
                pltpu.VMEM((2,) + cache.shape[1:], jnp.bfloat16),
                pltpu.SemaphoreType.DMA((2, 2)),
            ],
        ),
        out_shape=jax.ShapeDtypeStruct((steps, slots, heads, LAT), jnp.bfloat16),
        compiler_params=params(52),
        cost_estimate=cost(12),
        name="attend",
    )(lengths, receivers, queries, cache, moved, other, new_latent)


def pack_kernel(
    send_ref, token_hbm, id_hbm, affinity_hbm, cache_hbm, out_ref, moving_ref, token_ref, id_ref, affinity_ref, sems
):
    steps, requests, half_width = token_ref.shape
    topk = id_ref.shape[2]
    rows = steps * requests
    sending = send_ref[lax.axis_index("narrow"), 0] // (cache_hbm.shape[2] // 32)
    pairs = [
        (id_hbm, id_ref),
        (affinity_hbm, affinity_ref),
        (token_hbm, token_ref),
        (cache_hbm.at[sending, :, pl.ds(0, MOVED)], moving_ref),
    ]
    copies = [pltpu.make_async_copy(*pair, sems.at[index]) for index, pair in enumerate(pairs)]
    for copy in copies:
        copy.start()
    copies[0].wait()
    copies[1].wait()
    ids = id_ref[...].reshape(rows, topk)
    affinity = affinity_ref[...].reshape(rows, topk)
    share = route_scale * affinity / jnp.sum(affinity, axis=1, keepdims=True)
    high = share.astype(jnp.bfloat16).astype(jnp.float32)
    low = share - high
    lane = lax.broadcasted_iota(jnp.int32, (rows, 128), 1)
    hot = jnp.zeros((rows, 128), jnp.float32)
    shares = jnp.zeros((rows, 128), jnp.float32)
    for k in range(topk):
        named = ids[:, k : k + 1]
        hot = jnp.where(lane == named, 1.0, hot)
        shares = jnp.where(lane == named + 32, high[:, k : k + 1], shares)
        shares = jnp.where(lane == named + 64, low[:, k : k + 1], shares)
    row = lax.broadcasted_iota(jnp.int32, (rows, rows), 0)
    other = lax.broadcasted_iota(jnp.int32, (rows, rows), 1)
    earlier = ((other < row) & (row // requests == other // requests)).astype(jnp.bfloat16)
    before = jnp.dot(earlier, hot.astype(jnp.bfloat16), preferred_element_type=jnp.float32)
    routing = jnp.where(lane < 32, jnp.where(hot > 0.5, before, -1.0), shares).astype(jnp.bfloat16)
    copies[2].wait()
    out_ref[:, :half_width] = token_ref[...].reshape(rows, half_width)
    out_ref[:, half_width:] = routing
    copies[3].wait()


def pack(mig_send, tokens, expert_ids, affinity, keys_last):
    steps, requests, half_width = tokens.shape
    in_place = pl.BlockSpec(memory_space=pltpu.HBM)
    return pl.pallas_call(
        pack_kernel,
        in_specs=[pl.BlockSpec(memory_space=pltpu.SMEM)] + [in_place] * 4,
        out_specs=[IN_VMEM] * 2,
        out_shape=[
            jax.ShapeDtypeStruct((steps * requests, half_width + 128), jnp.bfloat16),
            jax.ShapeDtypeStruct((keys_last.shape[1], MOVED), jnp.bfloat16),
        ],
        scratch_shapes=[
            pltpu.VMEM(tokens.shape, jnp.bfloat16),
            pltpu.VMEM(expert_ids.shape, jnp.int32),
            pltpu.VMEM(affinity.shape, jnp.float32),
            pltpu.SemaphoreType.DMA((4,)),
        ],
        compiler_params=params(60),
        cost_estimate=cost(3),
        name="pack",
    )(mig_send, tokens, expert_ids, affinity, keys_last)


def stack_kernel(*refs):
    piece_refs, out_ref = refs[:SIDE], refs[SIDE]
    each = piece_refs[0].shape[0]
    for index, ref in enumerate(piece_refs):
        out_ref[index * each : (index + 1) * each, :] = ref[...]


def stack(pieces):
    rows, width = pieces[0].shape
    return pl.pallas_call(
        stack_kernel,
        in_specs=[IN_VMEM] * SIDE,
        out_specs=IN_VMEM,
        out_shape=jax.ShapeDtypeStruct((SIDE * rows, width), jnp.bfloat16),
        compiler_params=params(4),
        cost_estimate=cost(0.6),
        name="stack",
    )(*pieces)


def half_rows(refs, half, columns):
    each = refs[0].shape[0] // SIDE
    start = half * each // 2
    return jnp.concatenate(
        [
            ref[rank * each + start : rank * each + start + each // 2, columns]
            for ref in refs
            for rank in range(SIDE)
        ],
        axis=0,
    )


def four(rows, width):
    return [jax.ShapeDtypeStruct((rows, width), jnp.bfloat16)] * SIDE


def along_lanes(aux, wanted, shape, transposed):
    if transposed:
        lane = lax.broadcasted_iota(jnp.int32, (shape[0], 128), 1)
        chosen = (lane == wanted).astype(jnp.bfloat16)
        return lax.dot_general(
            chosen, aux, (((1,), (1,)), ((), ())), preferred_element_type=jnp.float32
        )
    lane = lax.broadcasted_iota(jnp.int32, (128, shape[1]), 0)
    chosen = (lane == wanted).astype(jnp.bfloat16)
    return jnp.dot(aux, chosen, preferred_element_type=jnp.float32)


def placed(aux, expert, shape, transposed):
    place = along_lanes(aux, expert, shape, transposed).astype(jnp.int32)
    row = lax.broadcasted_iota(jnp.int32, shape, 1 if transposed else 0)
    cell = lax.broadcasted_iota(jnp.int32, shape, 0 if transposed else 1)
    return (place >= 0) & (row // 8 * MOST + place == cell)


def pick_kernel(half, *refs):
    experts = reached_experts()
    piece_refs, out_refs = refs[:SIDE], refs[SIDE:]
    half_width = out_refs[0].shape[1]
    aux = half_rows(piece_refs, half, pl.ds(half_width, 128))
    rows = aux.shape[0]
    pickers = [
        placed(aux, experts[index], (rows // 2, rows), True).astype(jnp.bfloat16) for index in range(SIDE)
    ]
    for start in range(0, half_width, TILE):
        values = half_rows(piece_refs, half, pl.ds(start, TILE))
        for index in range(SIDE):
            out_refs[index][:, start : start + TILE] = jnp.dot(
                pickers[index], values, preferred_element_type=jnp.float32
            ).astype(jnp.bfloat16)


def pick(pieces, half, half_width):
    rows = pieces[0].shape[0] * SIDE // 2
    return pl.pallas_call(
        functools.partial(pick_kernel, half),
        in_specs=[IN_VMEM] * SIDE,
        out_specs=[IN_VMEM] * SIDE,
        out_shape=four(rows // 2, half_width),
        compiler_params=params(12),
        cost_estimate=cost(2),
        name="pick",
    )(*pieces)


def mix_kernel(half, by_inner, *refs):
    experts = reached_experts()
    piece_refs, cell_refs, out_refs = refs[:SIDE], refs[SIDE:-SIDE], refs[-SIDE:]
    rows_each, half_width = out_refs[0].shape
    rows = rows_each * SIDE
    cells = rows // 2
    each = rows_each // SIDE
    aux = half_rows(piece_refs, half, pl.ds(half_width, 128))
    mixers = []
    for index in range(SIDE):
        chosen = placed(aux, experts[index], (rows, cells), False)
        for level in (1, 2):
            share = along_lanes(aux, experts[index] + 32 * level, (rows, cells), False)
            mixers.append(jnp.where(chosen, share, 0.0).astype(jnp.bfloat16))
    high = jnp.concatenate(mixers[0::2], axis=1)
    low = jnp.concatenate(mixers[1::2], axis=1)
    for start in range(0, half_width, TILE):
        answers = jnp.concatenate(
            [ref[:, start : start + TILE] for ref in cell_refs], axis=0
        )
        mixed = jnp.dot(high, answers, preferred_element_type=jnp.float32)
        mixed = mixed + jnp.dot(low, answers, preferred_element_type=jnp.float32)
        mixed = mixed.astype(jnp.bfloat16)
        for outer in range(SIDE):
            for inner in range(SIDE):
                block = mixed[(outer * SIDE + inner) * each : (outer * SIDE + inner + 1) * each]
                piece, place = (inner, outer) if by_inner else (outer, inner)
                out_refs[piece][place * each : (place + 1) * each, start : start + TILE] = block


def mix(pieces, answers, half, by_inner):
    rows = pieces[0].shape[0] * SIDE // 2
    half_width = answers[0].shape[1]
    return pl.pallas_call(
        functools.partial(mix_kernel, half, by_inner),
        in_specs=[IN_VMEM] * 2 * SIDE,
        out_specs=[IN_VMEM] * SIDE,
        out_shape=four(rows // SIDE, half_width),
        compiler_params=params(16),
        cost_estimate=cost(2.5),
        name="mix",
    )(*pieces, *answers)


def widen_kernel(*refs):
    row_refs, (gate_ref, up_ref, *out_refs) = refs[:SIDE], refs[SIDE:]
    strides = block_strides()
    units = gate_ref.shape[1]
    rows = jnp.concatenate([ref[...] for ref in row_refs], axis=0)
    each = rows.shape[0] // SIDE**3
    for weight_ref, out_ref, sent_ref in zip((gate_ref, up_ref), out_refs[:2], out_refs[2:]):
        for start in range(0, units, 256):
            columns = pl.ds(start, 256)
            result = jnp.dot(
                rows, weight_ref[:, start : start + 256], preferred_element_type=jnp.float32
            )
            for outer in range(SIDE):
                for middle in range(SIDE):
                    for inner in range(SIDE):
                        block = (outer * SIDE + middle) * SIDE + inner
                        place = outer * strides[0] + middle * strides[1] + inner * strides[2]
                        place = pl.multiple_of(place * each, each)
                        out_ref[pl.ds(place, each), columns] = result[
                            block * each : (block + 1) * each
                        ]
            sent_ref[:, columns] = out_ref[:, columns].astype(jnp.bfloat16)


def widen(rows, gate_weight, up_weight):
    total = sum(array.shape[0] for array in rows)
    units = gate_weight.shape[1]
    return pl.pallas_call(
        widen_kernel,
        in_specs=[IN_VMEM] * (len(rows) + 2),
        out_specs=[IN_VMEM] * 4,
        out_shape=[
            jax.ShapeDtypeStruct((total, units), kind)
            for kind in (jnp.float32, jnp.float32, jnp.bfloat16, jnp.bfloat16)
        ],
        compiler_params=params(26),
        cost_estimate=cost(5),
        name="widen",
    )(*rows, gate_weight, up_weight)


def narrow_kernel(gate_own, up_own, gate_other, up_other, weight_ref, *refs):
    out_refs, hidden, wide = refs[:-2], *refs[-2:]
    strides = block_strides()
    units, half_width = weight_ref.shape
    total = wide.shape[0]
    cells, each = total // SIDE, total // SIDE**3
    wide[:, :units] = gate_own[...] + gate_other[...].astype(jnp.float32)
    wide[:, units:] = up_own[...] + up_other[...].astype(jnp.float32)
    for outer in range(SIDE):
        for middle in range(SIDE):
            parts = []
            for inner in range(SIDE):
                place = outer * strides[0] + middle * strides[1] + inner * strides[2]
                place = pl.ds(pl.multiple_of(place * each, each), each)
                gate = wide[place, :units]
                parts.append(gate / (1.0 + jnp.exp(-gate)) * wide[place, units:])
            block = (outer * SIDE + middle) * SIDE
            hidden[block * each : (block + SIDE) * each, :] = jnp.concatenate(
                parts, axis=0
            ).astype(jnp.bfloat16)
    for start in range(0, half_width, TILE):
        result = jnp.dot(
            hidden[...], weight_ref[:, start : start + TILE], preferred_element_type=jnp.float32
        )
        for index in range(SIDE):
            out_refs[index][:, start : start + TILE] = result[
                index * cells : (index + 1) * cells
            ].astype(jnp.bfloat16)


def narrow(gate_own, up_own, gate_other, up_other, down_weight):
    total = gate_own.shape[0]
    units, half_width = down_weight.shape
    return pl.pallas_call(
        narrow_kernel,
        in_specs=[IN_VMEM] * 5,
        out_specs=[IN_VMEM] * SIDE,
        out_shape=four(total // SIDE, half_width),
        scratch_shapes=[
            pltpu.VMEM((total, units), jnp.bfloat16),
            pltpu.VMEM((total, 2 * units), jnp.float32),
        ],
        compiler_params=params(20),
        cost_estimate=cost(3),
        name="narrow",
    )(gate_own, up_own, gate_other, up_other, down_weight)


def swap_cores(value):
    return lax.ppermute(value, "narrow", [(0, 1), (1, 0)])


def sum_kernel(*refs):
    piece_refs, out_refs = refs[:SIDE], refs[SIDE:]
    total = piece_refs[0][...].astype(jnp.float32)
    for ref in piece_refs[1:]:
        total = total + ref[...].astype(jnp.float32)
    total = total.astype(jnp.bfloat16)
    each = out_refs[0].shape[0]
    for index, out_ref in enumerate(out_refs):
        out_ref[...] = total[index * each : (index + 1) * each]


def add_up(pieces):
    rows, width = pieces[0].shape
    return pl.pallas_call(
        sum_kernel,
        in_specs=[IN_VMEM] * SIDE,
        out_specs=[IN_VMEM] * SIDE,
        out_shape=[jax.ShapeDtypeStruct((rows // SIDE, width), jnp.bfloat16)] * SIDE,
        compiler_params=params(8),
        name="add_up",
    )(*pieces)


def last_kernel(*refs):
    piece_refs, out_ref = refs[:-1], refs[-1]
    count = len(BATCHES)
    requests, width = out_ref.shape[1:]
    for batch in range(count):
        pieces = piece_refs[batch * SIDE : (batch + 1) * SIDE]
        total = pieces[0][...].astype(jnp.float32)
        for ref in pieces[1:]:
            total = total + ref[...].astype(jnp.float32)
        steps = total.shape[0] // requests
        out_ref[batch * steps : (batch + 1) * steps] = total.astype(jnp.bfloat16).reshape(
            steps, requests, width
        )


def add_last(pieces, shape):
    return pl.pallas_call(
        last_kernel,
        in_specs=[IN_VMEM] * len(pieces),
        out_specs=IN_VMEM,
        out_shape=jax.ShapeDtypeStruct(shape, jnp.bfloat16),
        compiler_params=params(6),
        name="add_last",
    )(*pieces)


def in_turn(earlier, later):
    return lax.optimization_barrier((earlier, later))


def body(
    cache,
    lengths,
    mig_send,
    mig_recv,
    mig_count,
    queries,
    new_latent,
    tokens,
    expert_ids,
    affinity,
    gate_weight,
    up_weight,
    down_weight,
):
    half_width = tokens.shape[2]

    def spread(stage, pieces):
        return [hop(piece, axes_at(stage), steps) for steps, piece in enumerate(pieces)]

    def bring(stage, pieces):
        return [hop(piece, axes_at(stage), -steps) for steps, piece in enumerate(pieces)]

    def answer(rows):
        gate, up, sent_gate, sent_up = widen(rows, gate_weight, up_weight)
        return narrow(gate, up, swap_cores(sent_gate), swap_cores(sent_up), down_weight)

    keys_last = jnp.swapaxes(cache, 1, 2)
    own_rows, moving = pack(mig_send[0], tokens, expert_ids, affinity, keys_last)
    pairs = [(r * 2 + j, (r + j + 1) % 64 * 2 + j) for r in range(64) for j in range(2)]
    moved = lax.ppermute(moving, BOTH, pairs)

    row = stack(spread(0, [own_rows] * SIDE))
    (moved, lengths), row = in_turn((moved, lengths), row)
    plane = spread(1, [row] * SIDE)
    context = attend(queries, keys_last, lengths, mig_recv[0], moved, swap_cores(moved), new_latent)
    context, plane = in_turn(context, plane)

    first_cells, second_cells = [spread(2, pick(plane, half, half_width)) for half in range(2)]

    first_answers = answer(first_cells)
    first_answers, second_cells = in_turn(first_answers, second_cells)
    first_answers = bring(2, first_answers)
    second_answers = bring(2, answer(second_cells))
    first = bring(1, add_up(bring(0, mix(plane, first_answers, 0, True))))
    second = bring(0, add_up(bring(1, mix(plane, second_answers, 1, False))))
    return (context, add_last(first + second, tokens.shape))


def solution(mesh):
    specs = (
        P("wide", None, None),
        P("wide"),
        P("wide", None, None),
        P("wide", None, None),
        P("wide", None),
        P(None, "wide", "narrow", None),
        P(None, "wide", None),
        P(None, "wide", "narrow"),
        P(None, "wide", None),
        P(None, "wide", None),
        P("narrow", "wide"),
        P("narrow", "wide"),
        P("wide", "narrow"),
    )
    return jax.shard_map(
        body,
        mesh=mesh,
        in_specs=specs,
        out_specs=(P(None, "wide", "narrow", None), P(None, "wide", "narrow")),
        check_vma=False,
    )
```

```python
import functools

import jax
import jax.numpy as jnp
from jax import lax
from jax.experimental import pallas as pl
from jax.experimental.pallas import tpu as pltpu
from jax.sharding import PartitionSpec as P

LAT = 512
STEPS = 4
MOST = 4
SIDE = 4
RANKS = SIDE * SIDE
MOVED = 256
TILE = 512
BATCHES = ((0, 1), (2, 3))
ORDERS = (("x", "y", "z"), ("x", "z", "y"))
STRIDE = {"z": 16, "y": 4, "x": 1}
BOTH = ("wide", "narrow")
MIB = 1024 * 1024
SHARE = 0.1


def cost(micros):
    return pl.CostEstimate(flops=int(micros * SHARE * 1.1e9), bytes_accessed=1, transcendentals=0)


IN_VMEM = pl.BlockSpec(memory_space=pltpu.VMEM)

score_scale = 192.0 ** (-0.5)
route_scale = 2.5


def params(mib):
    return pltpu.CompilerParams(vmem_limit_bytes=mib * MIB)


def moved_along(rank, axis, steps):
    place = rank // STRIDE[axis] % SIDE
    return rank + ((place + steps) % SIDE - place) * STRIDE[axis]


def hop(value, axes, steps):
    if steps == 0:
        return value
    pairs = [
        (rank * 2 + core, moved_along(rank, axes[core], steps) * 2 + core)
        for rank in range(64)
        for core in range(2)
    ]
    return lax.ppermute(value, BOTH, pairs)


def axes_at(stage):
    return tuple(order[stage] for order in ORDERS)


def by_core(core, first, second):
    return jnp.where(core == 0, first, second)


def reached_experts():
    rank, core = lax.axis_index("wide"), lax.axis_index("narrow")
    first, second = axes_at(2)
    return [
        by_core(core, moved_along(rank, first, steps) // 2, moved_along(rank, second, steps) // 2)
        for steps in range(SIDE)
    ]


def block_strides():
    core = lax.axis_index("narrow")
    return [by_core(core, *(STRIDE[axis] for axis in axes_at(level))) for level in (2, 1, 0)]


def attend_kernel(
    lengths, receivers, query_hbm, cache_hbm, moved_ref, other_ref, fresh_ref, out_ref, query_held, cache_held, sems
):
    slot = pl.program_id(0)
    count = pl.num_programs(0)

    def copies(index):
        held = lax.rem(index, 2)
        return (
            pltpu.make_async_copy(query_hbm.at[:, index], query_held.at[held], sems.at[held, 0]),
            pltpu.make_async_copy(cache_hbm.at[index], cache_held.at[held], sems.at[held, 1]),
        )

    @pl.when(slot == 0)
    def _():
        for copy in copies(slot):
            copy.start()

    @pl.when(slot + 1 < count)
    def _():
        for copy in copies(slot + 1):
            copy.start()

    for copy in copies(slot):
        copy.wait()
    now = lax.rem(slot, 2)
    query_ref, cache_ref = query_held.at[now], cache_held.at[now]
    length = lengths[slot]
    blocks = (length + 255) // 256
    steps, heads, width = query_ref.shape
    rows = steps * heads
    slots = fresh_ref.shape[1]
    core = lax.axis_index("narrow")
    per_slot = cache_ref.shape[1] // 32
    contract_last = (((1,), (1,)), ((), ()))

    def run(count):
        query = query_ref[...].reshape(rows, width)
        fresh = fresh_ref[...].reshape(-1, width)
        fresh_scores = (
            lax.dot_general(query, fresh, contract_last, preferred_element_type=jnp.float32)
            * score_scale
        )
        row_step = lax.broadcasted_iota(jnp.int32, fresh_scores.shape, 0) // heads
        column = lax.broadcasted_iota(jnp.int32, fresh_scores.shape, 1)
        allowed = (column // slots <= row_step) & (column % slots == slot)
        fresh_scores = jnp.where(allowed, fresh_scores, -jnp.inf)
        peak = jnp.max(fresh_scores, axis=1, keepdims=True)
        keys = []
        scores = []
        for index in range(count):
            key = cache_ref[:, index * 256 : (index + 1) * 256]
            if count == 1:
                key = jnp.where(slot == receivers[core, 0] // per_slot, moved_ref[...], key)
                key = jnp.where(slot == receivers[1 - core, 0] // per_slot, other_ref[...], key)
            score = jnp.dot(query, key, preferred_element_type=jnp.float32) * score_scale
            if index == count - 1:
                position = lax.broadcasted_iota(jnp.int32, score.shape, 1) + index * 256
                score = jnp.where(position < length, score, -jnp.inf)
            peak = jnp.maximum(peak, jnp.max(score, axis=1, keepdims=True))
            keys.append(key)
            scores.append(score)
        fresh_exp = jnp.exp(fresh_scores - peak)
        total = jnp.sum(fresh_exp, axis=1, keepdims=True)
        exps = []
        for score in scores:
            weight = jnp.exp(score - peak)
            total = total + jnp.sum(weight, axis=1, keepdims=True)
            exps.append(weight)
        inverse = 1.0 / total
        context = jnp.dot(
            (fresh_exp * inverse).astype(jnp.bfloat16),
            fresh[:, :LAT],
            preferred_element_type=jnp.float32,
        )
        for weight, key in zip(exps, keys):
            context = context + lax.dot_general(
                (weight * inverse).astype(jnp.bfloat16),
                key[:LAT],
                contract_last,
                preferred_element_type=jnp.float32,
            )
        out_ref[...] = context.astype(jnp.bfloat16).reshape(out_ref.shape)

    for count in range(5):
        pl.when(blocks == count)(functools.partial(run, count))


def attend(queries, cache, lengths, receivers, moved, other, new_latent):
    steps, slots, heads, width = queries.shape
    in_place = pl.BlockSpec(memory_space=pltpu.HBM)
    return pl.pallas_call(
        attend_kernel,
        grid_spec=pltpu.PrefetchScalarGridSpec(
            num_scalar_prefetch=2,
            grid=(slots,),
            in_specs=[in_place, in_place, IN_VMEM, IN_VMEM, IN_VMEM],
            out_specs=pl.BlockSpec((steps, 1, heads, LAT), lambda i, *_: (0, i, 0, 0)),
            scratch_shapes=[
                pltpu.VMEM((2, steps, heads, width), jnp.bfloat16),
                pltpu.VMEM((2,) + cache.shape[1:], jnp.bfloat16),
                pltpu.SemaphoreType.DMA((2, 2)),
            ],
        ),
        out_shape=jax.ShapeDtypeStruct((steps, slots, heads, LAT), jnp.bfloat16),
        compiler_params=params(52),
        cost_estimate=cost(12),
        name="attend",
    )(lengths, receivers, queries, cache, moved, other, new_latent)


def pack_kernel(
    send_ref, token_hbm, id_hbm, affinity_hbm, cache_hbm, out_ref, moving_ref, token_ref, id_ref, affinity_ref, sems
):
    steps, requests, half_width = token_ref.shape
    topk = id_ref.shape[2]
    rows = steps * requests
    sending = send_ref[lax.axis_index("narrow"), 0] // (cache_hbm.shape[2] // 32)
    pairs = [
        (id_hbm, id_ref),
        (affinity_hbm, affinity_ref),
        (token_hbm, token_ref),
        (cache_hbm.at[sending, :, pl.ds(0, MOVED)], moving_ref),
    ]
    copies = [pltpu.make_async_copy(*pair, sems.at[index]) for index, pair in enumerate(pairs)]
    for copy in copies:
        copy.start()
    copies[0].wait()
    copies[1].wait()
    ids = id_ref[...].reshape(rows, topk)
    affinity = affinity_ref[...].reshape(rows, topk)
    share = route_scale * affinity / jnp.sum(affinity, axis=1, keepdims=True)
    high = share.astype(jnp.bfloat16).astype(jnp.float32)
    low = share - high
    lane = lax.broadcasted_iota(jnp.int32, (rows, 128), 1)
    hot = jnp.zeros((rows, 128), jnp.float32)
    shares = jnp.zeros((rows, 128), jnp.float32)
    for k in range(topk):
        named = ids[:, k : k + 1]
        hot = jnp.where(lane == named, 1.0, hot)
        shares = jnp.where(lane == named + 32, high[:, k : k + 1], shares)
        shares = jnp.where(lane == named + 64, low[:, k : k + 1], shares)
    row = lax.broadcasted_iota(jnp.int32, (rows, rows), 0)
    other = lax.broadcasted_iota(jnp.int32, (rows, rows), 1)
    earlier = ((other < row) & (row // requests == other // requests)).astype(jnp.bfloat16)
    before = jnp.dot(earlier, hot.astype(jnp.bfloat16), preferred_element_type=jnp.float32)
    routing = jnp.where(lane < 32, jnp.where(hot > 0.5, before, -1.0), shares).astype(jnp.bfloat16)
    copies[2].wait()
    out_ref[:, :half_width] = token_ref[...].reshape(rows, half_width)
    out_ref[:, half_width:] = routing
    copies[3].wait()


def pack(mig_send, tokens, expert_ids, affinity, keys_last):
    steps, requests, half_width = tokens.shape
    in_place = pl.BlockSpec(memory_space=pltpu.HBM)
    return pl.pallas_call(
        pack_kernel,
        in_specs=[pl.BlockSpec(memory_space=pltpu.SMEM)] + [in_place] * 4,
        out_specs=[IN_VMEM] * 2,
        out_shape=[
            jax.ShapeDtypeStruct((steps * requests, half_width + 128), jnp.bfloat16),
            jax.ShapeDtypeStruct((keys_last.shape[1], MOVED), jnp.bfloat16),
        ],
        scratch_shapes=[
            pltpu.VMEM(tokens.shape, jnp.bfloat16),
            pltpu.VMEM(expert_ids.shape, jnp.int32),
            pltpu.VMEM(affinity.shape, jnp.float32),
            pltpu.SemaphoreType.DMA((4,)),
        ],
        compiler_params=params(60),
        cost_estimate=cost(3),
        name="pack",
    )(mig_send, tokens, expert_ids, affinity, keys_last)


def stack_kernel(*refs):
    piece_refs, out_ref = refs[:SIDE], refs[SIDE]
    each = piece_refs[0].shape[0]
    for index, ref in enumerate(piece_refs):
        out_ref[index * each : (index + 1) * each, :] = ref[...]


def stack(pieces):
    rows, width = pieces[0].shape
    return pl.pallas_call(
        stack_kernel,
        in_specs=[IN_VMEM] * SIDE,
        out_specs=IN_VMEM,
        out_shape=jax.ShapeDtypeStruct((SIDE * rows, width), jnp.bfloat16),
        compiler_params=params(4),
        cost_estimate=cost(0.6),
        name="stack",
    )(*pieces)


def half_rows(refs, half, columns):
    each = refs[0].shape[0] // SIDE
    start = half * each // 2
    return jnp.concatenate(
        [
            ref[rank * each + start : rank * each + start + each // 2, columns]
            for ref in refs
            for rank in range(SIDE)
        ],
        axis=0,
    )


def four(rows, width):
    return [jax.ShapeDtypeStruct((rows, width), jnp.bfloat16)] * SIDE


def along_lanes(aux, wanted, shape, transposed):
    if transposed:
        lane = lax.broadcasted_iota(jnp.int32, (shape[0], 128), 1)
        chosen = (lane == wanted).astype(jnp.bfloat16)
        return lax.dot_general(
            chosen, aux, (((1,), (1,)), ((), ())), preferred_element_type=jnp.float32
        )
    lane = lax.broadcasted_iota(jnp.int32, (128, shape[1]), 0)
    chosen = (lane == wanted).astype(jnp.bfloat16)
    return jnp.dot(aux, chosen, preferred_element_type=jnp.float32)


def placed(aux, expert, shape, transposed):
    place = along_lanes(aux, expert, shape, transposed).astype(jnp.int32)
    row = lax.broadcasted_iota(jnp.int32, shape, 1 if transposed else 0)
    cell = lax.broadcasted_iota(jnp.int32, shape, 0 if transposed else 1)
    return (place >= 0) & (row // 8 * MOST + place == cell)


def pick_kernel(half, *refs):
    experts = reached_experts()
    piece_refs, out_refs = refs[:SIDE], refs[SIDE:]
    half_width = out_refs[0].shape[1]
    aux = half_rows(piece_refs, half, pl.ds(half_width, 128))
    rows = aux.shape[0]
    pickers = [
        placed(aux, experts[index], (rows // 2, rows), True).astype(jnp.bfloat16) for index in range(SIDE)
    ]
    for start in range(0, half_width, TILE):
        values = half_rows(piece_refs, half, pl.ds(start, TILE))
        for index in range(SIDE):
            out_refs[index][:, start : start + TILE] = jnp.dot(
                pickers[index], values, preferred_element_type=jnp.float32
            ).astype(jnp.bfloat16)


def pick(pieces, half, half_width):
    rows = pieces[0].shape[0] * SIDE // 2
    return pl.pallas_call(
        functools.partial(pick_kernel, half),
        in_specs=[IN_VMEM] * SIDE,
        out_specs=[IN_VMEM] * SIDE,
        out_shape=four(rows // 2, half_width),
        compiler_params=params(12),
        cost_estimate=cost(2),
        name="pick",
    )(*pieces)


def mix_kernel(half, by_inner, *refs):
    experts = reached_experts()
    piece_refs, cell_refs, out_refs = refs[:SIDE], refs[SIDE:-SIDE], refs[-SIDE:]
    rows_each, half_width = out_refs[0].shape
    rows = rows_each * SIDE
    cells = rows // 2
    each = rows_each // SIDE
    aux = half_rows(piece_refs, half, pl.ds(half_width, 128))
    mixers = []
    for index in range(SIDE):
        chosen = placed(aux, experts[index], (rows, cells), False)
        for level in (1, 2):
            share = along_lanes(aux, experts[index] + 32 * level, (rows, cells), False)
            mixers.append(jnp.where(chosen, share, 0.0).astype(jnp.bfloat16))
    high = jnp.concatenate(mixers[0::2], axis=1)
    low = jnp.concatenate(mixers[1::2], axis=1)
    for start in range(0, half_width, TILE):
        answers = jnp.concatenate(
            [ref[:, start : start + TILE] for ref in cell_refs], axis=0
        )
        mixed = jnp.dot(high, answers, preferred_element_type=jnp.float32)
        mixed = mixed + jnp.dot(low, answers, preferred_element_type=jnp.float32)
        mixed = mixed.astype(jnp.bfloat16)
        for outer in range(SIDE):
            for inner in range(SIDE):
                block = mixed[(outer * SIDE + inner) * each : (outer * SIDE + inner + 1) * each]
                piece, place = (inner, outer) if by_inner else (outer, inner)
                out_refs[piece][place * each : (place + 1) * each, start : start + TILE] = block


def mix(pieces, answers, half, by_inner):
    rows = pieces[0].shape[0] * SIDE // 2
    half_width = answers[0].shape[1]
    return pl.pallas_call(
        functools.partial(mix_kernel, half, by_inner),
        in_specs=[IN_VMEM] * 2 * SIDE,
        out_specs=[IN_VMEM] * SIDE,
        out_shape=four(rows // SIDE, half_width),
        compiler_params=params(16),
        cost_estimate=cost(60),
        name="mix",
    )(*pieces, *answers)


def widen_kernel(*refs):
    row_refs, (gate_ref, up_ref, *out_refs) = refs[:SIDE], refs[SIDE:]
    strides = block_strides()
    units = gate_ref.shape[1]
    rows = jnp.concatenate([ref[...] for ref in row_refs], axis=0)
    each = rows.shape[0] // SIDE**3
    for weight_ref, out_ref, sent_ref in zip((gate_ref, up_ref), out_refs[:2], out_refs[2:]):
        for start in range(0, units, 256):
            columns = pl.ds(start, 256)
            result = jnp.dot(
                rows, weight_ref[:, start : start + 256], preferred_element_type=jnp.float32
            )
            for outer in range(SIDE):
                for middle in range(SIDE):
                    for inner in range(SIDE):
                        block = (outer * SIDE + middle) * SIDE + inner
                        place = outer * strides[0] + middle * strides[1] + inner * strides[2]
                        place = pl.multiple_of(place * each, each)
                        out_ref[pl.ds(place, each), columns] = result[
                            block * each : (block + 1) * each
                        ]
            sent_ref[:, columns] = out_ref[:, columns].astype(jnp.bfloat16)


def widen(rows, gate_weight, up_weight):
    total = sum(array.shape[0] for array in rows)
    units = gate_weight.shape[1]
    return pl.pallas_call(
        widen_kernel,
        in_specs=[IN_VMEM] * (len(rows) + 2),
        out_specs=[IN_VMEM] * 4,
        out_shape=[
            jax.ShapeDtypeStruct((total, units), kind)
            for kind in (jnp.float32, jnp.float32, jnp.bfloat16, jnp.bfloat16)
        ],
        compiler_params=params(26),
        cost_estimate=cost(5),
        name="widen",
    )(*rows, gate_weight, up_weight)


def narrow_kernel(gate_own, up_own, gate_other, up_other, weight_ref, *refs):
    out_refs, hidden, wide = refs[:-2], *refs[-2:]
    strides = block_strides()
    units, half_width = weight_ref.shape
    total = wide.shape[0]
    cells, each = total // SIDE, total // SIDE**3
    wide[:, :units] = gate_own[...] + gate_other[...].astype(jnp.float32)
    wide[:, units:] = up_own[...] + up_other[...].astype(jnp.float32)
    for outer in range(SIDE):
        for middle in range(SIDE):
            parts = []
            for inner in range(SIDE):
                place = outer * strides[0] + middle * strides[1] + inner * strides[2]
                place = pl.ds(pl.multiple_of(place * each, each), each)
                gate = wide[place, :units]
                parts.append(gate / (1.0 + jnp.exp(-gate)) * wide[place, units:])
            block = (outer * SIDE + middle) * SIDE
            hidden[block * each : (block + SIDE) * each, :] = jnp.concatenate(
                parts, axis=0
            ).astype(jnp.bfloat16)
    for start in range(0, half_width, TILE):
        result = jnp.dot(
            hidden[...], weight_ref[:, start : start + TILE], preferred_element_type=jnp.float32
        )
        for index in range(SIDE):
            out_refs[index][:, start : start + TILE] = result[
                index * cells : (index + 1) * cells
            ].astype(jnp.bfloat16)


def narrow(gate_own, up_own, gate_other, up_other, down_weight):
    total = gate_own.shape[0]
    units, half_width = down_weight.shape
    return pl.pallas_call(
        narrow_kernel,
        in_specs=[IN_VMEM] * 5,
        out_specs=[IN_VMEM] * SIDE,
        out_shape=four(total // SIDE, half_width),
        scratch_shapes=[
            pltpu.VMEM((total, units), jnp.bfloat16),
            pltpu.VMEM((total, 2 * units), jnp.float32),
        ],
        compiler_params=params(20),
        cost_estimate=cost(3),
        name="narrow",
    )(gate_own, up_own, gate_other, up_other, down_weight)


def swap_cores(value):
    return lax.ppermute(value, "narrow", [(0, 1), (1, 0)])


def sum_kernel(*refs):
    piece_refs, out_refs = refs[:SIDE], refs[SIDE:]
    total = piece_refs[0][...].astype(jnp.float32)
    for ref in piece_refs[1:]:
        total = total + ref[...].astype(jnp.float32)
    total = total.astype(jnp.bfloat16)
    each = out_refs[0].shape[0]
    for index, out_ref in enumerate(out_refs):
        out_ref[...] = total[index * each : (index + 1) * each]


def add_up(pieces):
    rows, width = pieces[0].shape
    return pl.pallas_call(
        sum_kernel,
        in_specs=[IN_VMEM] * SIDE,
        out_specs=[IN_VMEM] * SIDE,
        out_shape=[jax.ShapeDtypeStruct((rows // SIDE, width), jnp.bfloat16)] * SIDE,
        compiler_params=params(8),
        name="add_up",
    )(*pieces)


def last_kernel(*refs):
    piece_refs, out_ref = refs[:-1], refs[-1]
    count = len(BATCHES)
    requests, width = out_ref.shape[1:]
    for batch in range(count):
        pieces = piece_refs[batch * SIDE : (batch + 1) * SIDE]
        total = pieces[0][...].astype(jnp.float32)
        for ref in pieces[1:]:
            total = total + ref[...].astype(jnp.float32)
        steps = total.shape[0] // requests
        out_ref[batch * steps : (batch + 1) * steps] = total.astype(jnp.bfloat16).reshape(
            steps, requests, width
        )


def add_last(pieces, shape):
    return pl.pallas_call(
        last_kernel,
        in_specs=[IN_VMEM] * len(pieces),
        out_specs=IN_VMEM,
        out_shape=jax.ShapeDtypeStruct(shape, jnp.bfloat16),
        compiler_params=params(6),
        name="add_last",
    )(*pieces)


def in_turn(earlier, later):
    return lax.optimization_barrier((earlier, later))


def body(
    cache,
    lengths,
    mig_send,
    mig_recv,
    mig_count,
    queries,
    new_latent,
    tokens,
    expert_ids,
    affinity,
    gate_weight,
    up_weight,
    down_weight,
):
    half_width = tokens.shape[2]

    def spread(stage, pieces):
        return [hop(piece, axes_at(stage), steps) for steps, piece in enumerate(pieces)]

    def bring(stage, pieces):
        return [hop(piece, axes_at(stage), -steps) for steps, piece in enumerate(pieces)]

    def answer(rows):
        gate, up, sent_gate, sent_up = widen(rows, gate_weight, up_weight)
        return narrow(gate, up, swap_cores(sent_gate), swap_cores(sent_up), down_weight)

    keys_last = jnp.swapaxes(cache, 1, 2)
    own_rows, moving = pack(mig_send[0], tokens, expert_ids, affinity, keys_last)
    pairs = [(r * 2 + j, (r + j + 1) % 64 * 2 + j) for r in range(64) for j in range(2)]
    moved = lax.ppermute(moving, BOTH, pairs)

    row = stack(spread(0, [own_rows] * SIDE))
    (moved, lengths), row = in_turn((moved, lengths), row)
    plane = spread(1, [row] * SIDE)
    context = attend(queries, keys_last, lengths, mig_recv[0], moved, swap_cores(moved), new_latent)
    context, plane = in_turn(context, plane)

    first_cells, second_cells = [spread(2, pick(plane, half, half_width)) for half in range(2)]

    first_answers = answer(first_cells)
    first_answers, second_cells = in_turn(first_answers, second_cells)
    first_answers = bring(2, first_answers)
    second_answers = bring(2, answer(second_cells))
    first = bring(1, add_up(bring(0, mix(plane, first_answers, 0, True))))
    second = bring(0, add_up(bring(1, mix(plane, second_answers, 1, False))))
    return (context, add_last(first + second, tokens.shape))


def solution(mesh):
    specs = (
        P("wide", None, None),
        P("wide"),
        P("wide", None, None),
        P("wide", None, None),
        P("wide", None),
        P(None, "wide", "narrow", None),
        P(None, "wide", None),
        P(None, "wide", "narrow"),
        P(None, "wide", None),
        P(None, "wide", None),
        P("narrow", "wide"),
        P("narrow", "wide"),
        P("wide", "narrow"),
    )
    return jax.shard_map(
        body,
        mesh=mesh,
        in_specs=specs,
        out_specs=(P(None, "wide", "narrow", None), P(None, "wide", "narrow")),
        check_vma=False,
    )
```
